32 devices in a mesh: row: 4 (over z), col: 4 (over y, x), dp: 2 (over core).
Axes of the slice: x: 2, y: 2, z: 4, core: 2. Of those that a mesh axis runs over, the one named last changes fastest.
Arguments:
- tokens: bfloat16 [128, 8192], P(('col', 'dp'), 'row'), may hold values from -6 to 6
- grad_out: bfloat16 [128, 8192], P(('col', 'dp'), 'row'), may hold values from -1.1953125 to 1.1953125
- gate_weight: bfloat16 [8192, 16384], P('row', 'col'), may hold values from -0.0625 to 0.0625
- up_weight: bfloat16 [8192, 16384], P('row', 'col'), may hold values from -0.0625 to 0.0625
- down_weight: bfloat16 [16384, 8192], P('col', 'row'), may hold values from -0.046875 to 0.046875
Outputs:
- grad_tokens: bfloat16 [128, 8192], P(('col', 'dp'), 'row')
- grad_gate: bfloat16 [8192, 16384], P('row', ('col', 'dp'))
- grad_up: bfloat16 [8192, 16384], P('row', ('col', 'dp'))
- grad_down: bfloat16 [16384, 8192], P(('col', 'dp'), 'row')
The draws below stay inside these ranges and needn't reach their ends.
All inputs are finite; a program needn't handle non-finite values.
Results may differ from the reference program's by a relative error of at most 0.0049.
Values may be sent and summed in bfloat16 or wider, within the bound.
A program may use at most 128 MiB of HBM per device.

```python
import jax
import jax.numpy as jnp
from jax import lax

D = 8192
FFW = 16384
TOKENS = 128


def level_of(own_key, shape, shards, least, high):
    def one(dim, shards_of):
        heights = jax.random.uniform(jax.random.fold_in(jax.random.fold_in(own_key, 6), dim), (shards_of,), jnp.float32, least / len(shards), high / len(shards))
        return jnp.repeat(jnp.exp(heights), shape[dim] // shards_of).reshape((-1,) + (1,) * (len(shape) - dim - 1))

    factor_of = one(*shards[0])
    for cut in shards[1:]:
        factor_of = factor_of * one(*cut)
    return factor_of


def centred(own_key, shape, scale, limit, shards=(), held_as=jnp.bfloat16):
    entries = scale * jax.random.normal(own_key, shape, jnp.float32)
    if shards:
        entries = entries * level_of(own_key, shape, shards, -0.22, 0.18)
    return jnp.clip(entries, -limit, limit).astype(held_as)


def setup_inputs(seed: int = 0) -> dict:
    seeds = jax.random.split(jax.random.key(seed), 6)
    return {
        "tokens": centred(seeds[0], (TOKENS, D), 1.0, 6.0, ((0, 8), (1, 4))),
        "grad_out": centred(seeds[1], (TOKENS, D), 0.2, 1.1953125, ((0, 8), (1, 4))),
        "gate_weight": centred(seeds[2], (D, FFW), D ** -0.5, 0.0625, ((0, 4), (1, 4))),
        "up_weight": centred(seeds[3], (D, FFW), D ** -0.5, 0.0625, ((0, 4), (1, 4))),
        "down_weight": centred(seeds[4], (FFW, D), FFW ** -0.5, 0.046875, ((0, 4), (1, 4))),
    }


def reference(tokens, grad_out, gate_weight, up_weight, down_weight):
    contract_last = (((1,), (1,)), ((), ()))
    contract_first = (((0,), (0,)), ((), ()))
    gate = jnp.dot(tokens, gate_weight, preferred_element_type=jnp.float32)
    up = jnp.dot(tokens, up_weight, preferred_element_type=jnp.float32)
    grad_hidden = lax.dot_general(grad_out, down_weight, contract_last, preferred_element_type=jnp.float32)
    sig = jax.nn.sigmoid(gate)
    hidden = (gate * sig * up).astype(jnp.bfloat16)
    grad_g = (grad_hidden * up * sig * (1.0 + gate * (1.0 - sig))).astype(jnp.bfloat16)
    grad_u = (grad_hidden * gate * sig).astype(jnp.bfloat16)
    grad_tokens = lax.dot_general(grad_g, gate_weight, contract_last, preferred_element_type=jnp.float32)
    grad_tokens = grad_tokens + lax.dot_general(grad_u, up_weight, contract_last, preferred_element_type=jnp.float32)
    grad_gate = lax.dot_general(tokens, grad_g, contract_first, preferred_element_type=jnp.float32)
    grad_up = lax.dot_general(tokens, grad_u, contract_first, preferred_element_type=jnp.float32)
    grad_down = lax.dot_general(hidden, grad_out, contract_first, preferred_element_type=jnp.float32)
    return (grad_tokens.astype(jnp.bfloat16), grad_gate.astype(jnp.bfloat16),
            grad_up.astype(jnp.bfloat16), grad_down.astype(jnp.bfloat16))
```

```python
import functools

import jax
import jax.numpy as jnp
from jax import lax
from jax.experimental import pallas as pl
from jax.experimental.pallas import tpu as pltpu
from jax.sharding import PartitionSpec as P

MESH = pl.DeviceIdType.MESH
BF16 = jnp.bfloat16
F32 = jnp.float32
NT = (((1,), (1,)), ((), ()))
TN = (((0,), (0,)), ((), ()))


def swiglu_back(gate, up, grad_hidden):
    sig = jax.nn.sigmoid(gate)
    hidden = (gate * sig * up).astype(BF16)
    grad_g = (grad_hidden * up * sig * (1.0 + gate * (1.0 - sig))).astype(BF16)
    grad_u = (grad_hidden * gate * sig).astype(BF16)
    return (hidden, grad_g, grad_u)


def exchange(
    n_row, n_col, nc, wire,
    tok_in, go_in, wg_in, wu_in, wd_in,
    gt_out, tok_out, go_out, h_out, g_out, u_out,
    x_v, wg_v, wu_v, wd_v, send_v, acc_v, mid_v, sum_v, res_v, gt_v, sib_v, peer_src, peer_v,
    w_sem, own_sem, out_sem,
    k_send, k_recv, s_send, s_recv,
    p_send, p_recv, m_recv, r_send, r_recv,
    t_send, t_recv, q_send, q_recv,
):
    row, col, dp = lax.axis_index("row"), lax.axis_index("col"), lax.axis_index("dp")
    rows, feats = tok_in.shape
    chunk = wg_v.shape[2]
    hid = nc * chunk
    half = n_row // 2
    left = row < half
    inner = jnp.where(left, row + 1, row - 1)
    outer = jnp.where(left, row - 1, row + 1)
    edge = jnp.logical_or(row == 0, row == n_row - 1)
    middle = jnp.logical_or(row == half - 1, row == half)
    off = dp * hid

    def block(j, core):
        return pl.ds(pl.multiple_of((j * 2 + core) * rows, 16), rows)

    def columns(c, base=0):
        return pl.ds(pl.multiple_of(base + c * chunk, 128), chunk)

    def weight_copies(c):
        return (
            pltpu.make_async_copy(wg_in.at[:, columns(c, off)], wg_v.at[c], w_sem.at[c, 0]),
            pltpu.make_async_copy(wu_in.at[:, columns(c, off)], wu_v.at[c], w_sem.at[c, 1]),
            pltpu.make_async_copy(wd_in.at[columns(c, off)], wd_v.at[c], w_sem.at[c, 2]),
        )

    own = [
        pltpu.make_async_copy(src, x_v.at[a, block(col, dp)], own_sem.at[a])
        for a, src in enumerate((tok_in, go_in))
    ]
    for copy in own:
        copy.start()

    def load(c, carry):
        for copy in weight_copies(c):
            copy.start()
        return carry

    lax.fori_loop(0, nc, load, 0)

    def col_at(k):
        return lax.rem(col + k, n_col)

    barrier = pltpu.get_barrier_semaphore()
    for k in range(1, n_col):
        pl.semaphore_signal(barrier, inc=1, device_id=(row, col_at(k), dp), device_id_type=MESH)
    pl.semaphore_signal(barrier, inc=1, device_id=(row, col, 1 - dp), device_id_type=MESH)
    pl.semaphore_signal(barrier, inc=1, device_id=(inner, col, dp), device_id_type=MESH)

    @pl.when(jnp.logical_not(edge))
    def _():
        pl.semaphore_signal(barrier, inc=1, device_id=(outer, col, dp), device_id_type=MESH)
        pl.semaphore_wait(barrier, n_col + 2)

    @pl.when(edge)
    def _():
        pl.semaphore_wait(barrier, n_col + 1)

    def to_peer(k, a):
        return pltpu.make_async_remote_copy(
            src_ref=(tok_in, go_in)[a],
            dst_ref=x_v.at[a, block(col, dp)],
            send_sem=k_send.at[k, a],
            recv_sem=k_recv.at[k, a],
            device_id=(row, col_at(k), dp),
            device_id_type=MESH,
        )

    def to_sibling(k, a):
        rows_of = block(col_at(n_col - k), dp)
        return pltpu.make_async_remote_copy(
            src_ref=(tok_in, go_in)[a] if k == 0 else x_v.at[a, rows_of],
            dst_ref=x_v.at[a, rows_of],
            send_sem=s_send.at[k, a],
            recv_sem=s_recv.at[k, a],
            device_id=(row, col, 1 - dp),
            device_id_type=MESH,
        )

    for a in range(2):
        for k in range(1, n_col):
            to_peer(k, a).start()
        to_sibling(0, a).start()
    for a in range(2):
        for k in range(1, n_col):
            to_peer(k, a).wait_recv()
            to_sibling(k, a).start()
    for copy in own:
        copy.wait()
    for a in range(2):
        for k in range(n_col):
            to_sibling(k, a).wait_recv()
    x_out = [
        pltpu.make_async_copy(x_v.at[a], dst, own_sem.at[a])
        for a, dst in enumerate((tok_out, go_out))
    ]
    for copy in x_out:
        copy.start()

    def sum_inwards(c, into_middle):
        return pltpu.make_async_remote_copy(
            src_ref=send_v.at[c],
            dst_ref=mid_v.at[c] if into_middle else acc_v.at[c],
            send_sem=p_send.at[c],
            recv_sem=m_recv.at[c] if into_middle else p_recv.at[c],
            device_id=(inner, col, dp),
            device_id_type=MESH,
        )

    def result_outwards(c):
        return pltpu.make_async_remote_copy(
            src_ref=res_v.at[c],
            dst_ref=res_v.at[c],
            send_sem=r_send.at[c],
            recv_sem=r_recv.at[c],
            device_id=(outer, col, dp),
            device_id_type=MESH,
        )

    def result_copies(c):
        return [
            pltpu.make_async_copy(res_v.at[c, i], dst.at[:, columns(c)], out_sem.at[c, i])
            for i, dst in enumerate((h_out, g_out, u_out))
        ]

    gt_v[...] = jnp.zeros_like(gt_v)

    def backward(c):
        for copy in result_copies(c):
            copy.start()
        gt_v[...] += lax.dot_general(
            res_v[c, 1], wg_v[c], NT, preferred_element_type=F32
        ) + lax.dot_general(res_v[c, 2], wu_v[c], NT, preferred_element_type=F32)

    def finish(c):
        sum_inwards(c, True).wait_recv()
        h, g, u = swiglu_back(*(sum_v[c, i] + mid_v[c, i].astype(F32) for i in range(3)))
        res_v[c, 0] = h
        res_v[c, 1] = g
        res_v[c, 2] = u
        if half > 1:
            result_outwards(c).start()
        backward(c)

    def forward(c, carry):
        for copy in weight_copies(c):
            copy.wait()
        sum_v[c, 0] = jnp.dot(x_v[0], wg_v[c], preferred_element_type=F32)
        sum_v[c, 1] = jnp.dot(x_v[0], wu_v[c], preferred_element_type=F32)
        sum_v[c, 2] = lax.dot_general(x_v[1], wd_v[c], NT, preferred_element_type=F32)

        if half > 1:

            @pl.when(jnp.logical_not(edge))
            def _():
                sum_inwards(c, False).wait_recv()
                sum_v[c] += acc_v[c].astype(F32)

        send_v[c] = sum_v[c].astype(wire)

        @pl.when(middle)
        def _():
            sum_inwards(c, True).start()

            @pl.when(c > 0)
            def _():
                finish(c - 1)

        @pl.when(jnp.logical_not(middle))
        def _():
            sum_inwards(c, False).start()

        return carry

    lax.fori_loop(0, nc, forward, 0)

    @pl.when(middle)
    def _():
        finish(nc - 1)

    if half > 1:

        @pl.when(jnp.logical_not(middle))
        def _():
            def take(c, carry):
                result_outwards(c).wait_recv()

                @pl.when(jnp.logical_not(edge))
                def _():
                    result_outwards(c).start()

                backward(c)
                return carry

            lax.fori_loop(0, nc, take, 0)

    def half_to_sibling(k):
        return pltpu.make_async_remote_copy(
            src_ref=gt_v.at[block(col_at(k), 1 - dp)],
            dst_ref=sib_v.at[k],
            send_sem=t_send.at[k],
            recv_sem=t_recv.at[k],
            device_id=(row, col, 1 - dp),
            device_id_type=MESH,
        )

    def block_to_owner(k):
        return pltpu.make_async_remote_copy(
            src_ref=peer_src.at[k],
            dst_ref=peer_v.at[k],
            send_sem=q_send.at[k],
            recv_sem=q_recv.at[k],
            device_id=(row, col_at(k), dp),
            device_id_type=MESH,
        )

    order = list(range(1, n_col)) + [0]
    for k in order:
        half_to_sibling(k).start()
    for k in order[:-1]:
        half_to_sibling(k).wait_recv()
        peer_src[k] = (gt_v[block(col_at(k), dp), :] + sib_v[k]).astype(wire)
        block_to_owner(k).start()
    half_to_sibling(0).wait_recv()
    total = gt_v[block(col, dp), :] + sib_v[0]
    for k in order[:-1]:
        block_to_owner(k).wait_recv()
        total = total + peer_v[k].astype(F32)
    gt_out[...] = total.astype(BF16)

    for k in order:
        half_to_sibling(k).wait_send()
    for k in order[:-1]:
        block_to_owner(k).wait_send()
    for a in range(2):
        x_out[a].wait()
        for k in range(n_col):
            to_sibling(k, a).wait_send()
            if k > 0:
                to_peer(k, a).wait_send()

    def drain(c, carry):
        for copy in result_copies(c):
            copy.wait()
        sum_inwards(c, False).wait_send()
        if half > 1:

            @pl.when(jnp.logical_not(edge))
            def _():
                result_outwards(c).wait_send()

        return carry

    lax.fori_loop(0, nc, drain, 0)


def outer_products(tok, go, h, g, u, gate_out, up_out, down_out):
    gate_out[...] = lax.dot_general(
        tok[...], g[...], TN, preferred_element_type=F32
    ).astype(BF16)
    up_out[...] = lax.dot_general(tok[...], u[...], TN, preferred_element_type=F32).astype(BF16)
    down_out[...] = lax.dot_general(h[...], go[...], TN, preferred_element_type=F32).astype(BF16)


def body(n_row, n_col, tokens, grad_out, gate_weight, up_weight, down_weight):
    rows, feats = tokens.shape
    panel = rows * n_col * 2
    hid = gate_weight.shape[1] // 2
    chunk = min(256, hid)
    nc = hid // chunk
    wire = BF16 if n_row <= 4 else F32
    anywhere = pl.BlockSpec(memory_space=pl.ANY)
    dma = pltpu.SemaphoreType.DMA
    grad_tokens, tok, go, h, g, u = pl.pallas_call(
        functools.partial(exchange, n_row, n_col, nc, wire),
        out_shape=[
            jax.ShapeDtypeStruct((rows, feats), BF16),
            jax.ShapeDtypeStruct((panel, feats), BF16),
            jax.ShapeDtypeStruct((panel, feats), BF16),
            jax.ShapeDtypeStruct((panel, hid), BF16),
            jax.ShapeDtypeStruct((panel, hid), BF16),
            jax.ShapeDtypeStruct((panel, hid), BF16),
        ],
        in_specs=[anywhere] * 5,
        out_specs=[pl.BlockSpec(memory_space=pltpu.VMEM)] + [anywhere] * 5,
        scratch_shapes=[
            pltpu.VMEM((2, panel, feats), BF16),
            pltpu.VMEM((nc, feats, chunk), BF16),
            pltpu.VMEM((nc, feats, chunk), BF16),
            pltpu.VMEM((nc, chunk, feats), BF16),
            pltpu.VMEM((nc, 3, panel, chunk), wire),
            pltpu.VMEM((nc, 3, panel, chunk), wire),
            pltpu.VMEM((nc, 3, panel, chunk), wire),
            pltpu.VMEM((nc, 3, panel, chunk), F32),
            pltpu.VMEM((nc, 3, panel, chunk), BF16),
            pltpu.VMEM((panel, feats), F32),
            pltpu.VMEM((n_col, rows, feats), F32),
            pltpu.VMEM((n_col, rows, feats), wire),
            pltpu.VMEM((n_col, rows, feats), wire),
            dma((nc, 3)), dma((2,)), dma((nc, 3)),
            dma((n_col, 2)), dma((n_col, 2)), dma((n_col, 2)), dma((n_col, 2)),
            dma((nc,)), dma((nc,)), dma((nc,)), dma((nc,)), dma((nc,)),
            dma((n_col,)), dma((n_col,)), dma((n_col,)), dma((n_col,)),
        ],
        compiler_params=pltpu.CompilerParams(
            collective_id=0, has_side_effects=True, vmem_limit_bytes=56 * 2**20
        ),
        name="exchange",
    )(tokens, grad_out, gate_weight, up_weight, down_weight)

    nb = max(1, feats // 256)
    whole = lambda i: (0, 0)
    cut = lambda i: (0, i)
    stack = lambda i: (i, 0)
    grad_gate, grad_up, grad_down = pl.pallas_call(
        outer_products,
        grid=(nb,),
        in_specs=[
            pl.BlockSpec((panel, feats // nb), cut),
            pl.BlockSpec((panel, feats), whole),
            pl.BlockSpec((panel, hid // nb), cut),
            pl.BlockSpec((panel, hid), whole),
            pl.BlockSpec((panel, hid), whole),
        ],
        out_specs=[
            pl.BlockSpec((feats // nb, hid), stack),
            pl.BlockSpec((feats // nb, hid), stack),
            pl.BlockSpec((hid // nb, feats), stack),
        ],
        out_shape=[
            jax.ShapeDtypeStruct((feats, hid), BF16),
            jax.ShapeDtypeStruct((feats, hid), BF16),
            jax.ShapeDtypeStruct((hid, feats), BF16),
        ],
        compiler_params=pltpu.CompilerParams(vmem_limit_bytes=40 * 2**20),
        name="outer_products",
    )(tok, go, h, g, u)
    return (grad_tokens, grad_gate, grad_up, grad_down)


def solution(mesh):
    in_specs = (
        P(("col", "dp"), "row"),
        P(("col", "dp"), "row"),
        P("row", "col"),
        P("row", "col"),
        P("col", "row"),
    )
    out_specs = (
        P(("col", "dp"), "row"),
        P("row", ("col", "dp")),
        P("row", ("col", "dp")),
        P(("col", "dp"), "row"),
    )
    run = functools.partial(body, mesh.shape["row"], mesh.shape["col"])
    return jax.shard_map(run, mesh=mesh, in_specs=in_specs, out_specs=out_specs, check_vma=False)
```

```python
import functools

import jax
import jax.numpy as jnp
from jax import lax
from jax.experimental import pallas as pl
from jax.experimental.pallas import tpu as pltpu
from jax.sharding import PartitionSpec as P

MESH = pl.DeviceIdType.MESH
BF16 = jnp.bfloat16
F32 = jnp.float32
NT = (((1,), (1,)), ((), ()))


def swiglu_back(gate, up, grad_hidden):
    sig = jax.nn.sigmoid(gate)
    hidden = (gate * sig * up).astype(BF16)
    grad_g = (grad_hidden * up * sig * (1.0 + gate * (1.0 - sig))).astype(BF16)
    grad_u = (grad_hidden * gate * sig).astype(BF16)
    return (hidden, grad_g, grad_u)


def exchange(
    n_row, n_col, nc, ns, wire,
    tok_in, go_in, wg_in, wu_in, wd_in,
    gt_out, tok_out, go_out, h_out, g_out, u_out,
    x_v, wg_v, wu_v, wd_v, send_v, acc_v, mid_v, sum_v, res_v, gt_v, sib_v, peer_src, peer_v,
    turn_v, hid_v,
    w_sem, own_sem, out_sem,
    k_send, k_recv, s_send, s_recv,
    p_send, p_recv, m_recv, r_send, r_recv,
    t_send, t_recv, q_send, q_recv,
):
    row, col, dp = lax.axis_index("row"), lax.axis_index("col"), lax.axis_index("dp")
    rows, feats = tok_in.shape
    panel = x_v.shape[1]
    chunk = wg_v.shape[2]
    hid = nc * chunk
    half = n_row // 2
    left = row < half
    inner = jnp.where(left, row + 1, row - 1)
    outer = jnp.where(left, row - 1, row + 1)
    edge = jnp.logical_or(row == 0, row == n_row - 1)
    middle = jnp.logical_or(row == half - 1, row == half)
    off = dp * hid

    first = 2 * rows
    step = (panel - first) // ns
    units = [(0, first)] + [(first + i * step, step) for i in range(ns)]

    def block(k, core):
        return pl.ds(pl.multiple_of((k * 2 + core) * rows, 16), rows)

    def columns(c, base=0):
        return pl.ds(pl.multiple_of(base + c * chunk, 128), chunk)

    def weight_copies(c):
        return (
            pltpu.make_async_copy(wg_in.at[:, columns(c, off)], wg_v.at[c], w_sem.at[c, 0]),
            pltpu.make_async_copy(wu_in.at[:, columns(c, off)], wu_v.at[c], w_sem.at[c, 1]),
            pltpu.make_async_copy(wd_in.at[columns(c, off)], wd_v.at[c], w_sem.at[c, 2]),
        )

    own = [
        pltpu.make_async_copy(src, x_v.at[a, block(0, dp)], own_sem.at[a])
        for a, src in enumerate((tok_in, go_in))
    ]
    for copy in own:
        copy.start()

    def load(c, carry):
        for copy in weight_copies(c):
            copy.start()
        return carry

    lax.fori_loop(0, nc, load, 0)

    def col_at(k):
        return lax.rem(col + k, n_col)

    barrier = pltpu.get_barrier_semaphore()
    for k in range(1, n_col):
        pl.semaphore_signal(barrier, inc=1, device_id=(row, col_at(k), dp), device_id_type=MESH)
    pl.semaphore_signal(barrier, inc=1, device_id=(row, col, 1 - dp), device_id_type=MESH)
    pl.semaphore_signal(barrier, inc=1, device_id=(inner, col, dp), device_id_type=MESH)

    @pl.when(jnp.logical_not(edge))
    def _():
        pl.semaphore_signal(barrier, inc=1, device_id=(outer, col, dp), device_id_type=MESH)
        pl.semaphore_wait(barrier, n_col + 2)

    @pl.when(edge)
    def _():
        pl.semaphore_wait(barrier, n_col + 1)

    def to_peer(k, a):
        return pltpu.make_async_remote_copy(
            src_ref=(tok_in, go_in)[a],
            dst_ref=x_v.at[a, block(n_col - k, dp)],
            send_sem=k_send.at[k, a],
            recv_sem=k_recv.at[k, a],
            device_id=(row, col_at(k), dp),
            device_id_type=MESH,
        )

    def to_sibling(k, a):
        return pltpu.make_async_remote_copy(
            src_ref=(tok_in, go_in)[a] if k == 0 else x_v.at[a, block(k, dp)],
            dst_ref=x_v.at[a, block(k, dp)],
            send_sem=s_send.at[k, a],
            recv_sem=s_recv.at[k, a],
            device_id=(row, col, 1 - dp),
            device_id_type=MESH,
        )

    for a in range(2):
        to_sibling(0, a).start()
    for a in range(2):
        for k in range(1, n_col):
            to_peer(k, a).start()

    def part(ref, c, t):
        return ref.at[c, :, pl.ds(*units[t])]

    def sum_inwards(c, t, into_middle):
        return pltpu.make_async_remote_copy(
            src_ref=part(send_v, c, t),
            dst_ref=part(mid_v if into_middle else acc_v, c, t),
            send_sem=p_send.at[c, t],
            recv_sem=(m_recv if into_middle else p_recv).at[c, t],
            device_id=(inner, col, dp),
            device_id_type=MESH,
        )

    def result_outwards(c, t):
        return pltpu.make_async_remote_copy(
            src_ref=part(res_v, c, t),
            dst_ref=part(res_v, c, t),
            send_sem=r_send.at[c, t],
            recv_sem=r_recv.at[c, t],
            device_id=(outer, col, dp),
            device_id_type=MESH,
        )

    def result_copies(c):
        return [
            pltpu.make_async_copy(hid_v.at[c], h_out.at[columns(c)], out_sem.at[c, 0]),
            pltpu.make_async_copy(res_v.at[c, 1], g_out.at[:, columns(c)], out_sem.at[c, 1]),
            pltpu.make_async_copy(res_v.at[c, 2], u_out.at[:, columns(c)], out_sem.at[c, 2]),
        ]

    gt_v[...] = jnp.zeros_like(gt_v)

    def backward(c):
        hid_v[c] = res_v[c, 0].T
        for copy in result_copies(c):
            copy.start()
        gt_v[...] += lax.dot_general(
            res_v[c, 1], wg_v[c], NT, preferred_element_type=F32
        ) + lax.dot_general(res_v[c, 2], wu_v[c], NT, preferred_element_type=F32)

    def finish(c, t):
        sum_inwards(c, t, True).wait_recv()
        at = pl.ds(*units[t])
        h, g, u = swiglu_back(*(sum_v[c, i, at] + mid_v[c, i, at].astype(F32) for i in range(3)))
        res_v[c, 0, at] = h
        res_v[c, 1, at] = g
        res_v[c, 2, at] = u
        if half > 1:
            result_outwards(c, t).start()
        if t == ns:
            backward(c)

    def forward(c, start, count):
        at = pl.ds(start, count)
        sum_v[c, 0, at] = jnp.dot(x_v[0, at], wg_v[c], preferred_element_type=F32)
        sum_v[c, 1, at] = jnp.dot(x_v[0, at], wu_v[c], preferred_element_type=F32)
        sum_v[c, 2, at] = lax.dot_general(x_v[1, at], wd_v[c], NT, preferred_element_type=F32)

    def send_on(c, t, then):
        at = pl.ds(*units[t])
        if half > 1:

            @pl.when(jnp.logical_not(edge))
            def _():
                sum_inwards(c, t, False).wait_recv()
                sum_v[c, :, at] += acc_v[c, :, at].astype(F32)

        send_v[c, :, at] = sum_v[c, :, at].astype(wire)

        @pl.when(middle)
        def _():
            sum_inwards(c, t, True).start()
            then()

        @pl.when(jnp.logical_not(middle))
        def _():
            sum_inwards(c, t, False).start()

    for copy in own:
        copy.wait()
    for a in range(2):
        to_sibling(0, a).wait_recv()

    def near(c, carry):
        for copy in weight_copies(c):
            copy.wait()
        forward(c, 0, first)

        def then():
            @pl.when(c > 1)
            def _():
                finish(c - 2, 0)

        send_on(c, 0, then)

        @pl.when(c == nc - 2)
        def _():
            for a in range(2):
                for k in range(1, n_col):
                    to_peer(n_col - k, a).wait_recv()
                    to_sibling(k, a).start()

        return carry

    lax.fori_loop(0, nc, near, 0)

    for a in range(2):
        for k in range(1, n_col):
            to_sibling(k, a).wait_recv()

    def far(c, carry):
        forward(c, first, panel - first)
        for t in range(1, ns + 1):

            def then(t=t):
                if t > 2:
                    finish(c, t - 2)
                else:

                    @pl.when(c == 0)
                    def _():
                        finish(nc - 3 + t, 0)

                    @pl.when(c > 0)
                    def _():
                        finish(c - 1, ns - 2 + t)

            send_on(c, t, then)
        return carry

    lax.fori_loop(0, nc, far, 0)

    turn_v[...] = x_v[0].T
    x_out = [
        pltpu.make_async_copy(turn_v, tok_out, own_sem.at[0]),
        pltpu.make_async_copy(x_v.at[1], go_out, own_sem.at[1]),
    ]
    for copy in x_out:
        copy.start()

    @pl.when(middle)
    def _():
        finish(nc - 1, ns - 1)
        finish(nc - 1, ns)

    if half > 1:

        @pl.when(jnp.logical_not(middle))
        def _():
            def take(c, t):
                result_outwards(c, t).wait_recv()

                @pl.when(jnp.logical_not(edge))
                def _():
                    result_outwards(c, t).start()

            def take_near(c, carry):
                take(c, 0)
                return carry

            def take_far(c, carry):
                for t in range(1, ns + 1):
                    take(c, t)
                backward(c)
                return carry

            lax.fori_loop(0, nc, take_near, 0)
            lax.fori_loop(0, nc, take_far, 0)

    def half_to_sibling(k):
        return pltpu.make_async_remote_copy(
            src_ref=gt_v.at[block(k, 1 - dp)],
            dst_ref=sib_v.at[k],
            send_sem=t_send.at[k],
            recv_sem=t_recv.at[k],
            device_id=(row, col, 1 - dp),
            device_id_type=MESH,
        )

    def block_to_owner(k):
        return pltpu.make_async_remote_copy(
            src_ref=peer_src.at[k],
            dst_ref=peer_v.at[k],
            send_sem=q_send.at[k],
            recv_sem=q_recv.at[k],
            device_id=(row, col_at(k), dp),
            device_id_type=MESH,
        )

    order = list(range(1, n_col)) + [0]
    for k in order:
        half_to_sibling(k).start()
    for k in order[:-1]:
        half_to_sibling(k).wait_recv()
        peer_src[k] = (gt_v[block(k, dp), :] + sib_v[k]).astype(wire)
        block_to_owner(k).start()
    half_to_sibling(0).wait_recv()
    total = gt_v[block(0, dp), :] + sib_v[0]
    for k in order[:-1]:
        block_to_owner(k).wait_recv()
        total = total + peer_v[k].astype(F32)
    gt_out[...] = total.astype(BF16)

    for k in order:
        half_to_sibling(k).wait_send()
    for k in order[:-1]:
        block_to_owner(k).wait_send()
    for a in range(2):
        x_out[a].wait()
        for k in range(n_col):
            to_sibling(k, a).wait_send()
            if k > 0:
                to_peer(k, a).wait_send()

    def drain(c, carry):
        for copy in result_copies(c):
            copy.wait()
        for t in range(ns + 1):
            sum_inwards(c, t, False).wait_send()
            if half > 1:

                @pl.when(jnp.logical_not(edge))
                def _():
                    result_outwards(c, t).wait_send()

        return carry

    lax.fori_loop(0, nc, drain, 0)


def outer_products(grad_in, tok, go, h, g, u, grad_tokens, gate_out, up_out, down_out):
    @pl.when(pl.program_id(0) == 0)
    def _():
        grad_tokens[...] = grad_in[...]

    gate_out[...] = jnp.dot(tok[...], g[...], preferred_element_type=F32).astype(BF16)
    up_out[...] = jnp.dot(tok[...], u[...], preferred_element_type=F32).astype(BF16)
    down_out[...] = jnp.dot(h[...], go[...], preferred_element_type=F32).astype(BF16)


def body(n_row, n_col, tokens, grad_out, gate_weight, up_weight, down_weight):
    rows, feats = tokens.shape
    panel = rows * n_col * 2
    hid = gate_weight.shape[1] // 2
    chunk = min(256, hid // 2)
    nc = hid // chunk
    ns = 3 if (panel - 2 * rows) % 48 == 0 else 2
    wire = BF16 if n_row <= 4 else F32
    anywhere = pl.BlockSpec(memory_space=pl.ANY)
    dma = pltpu.SemaphoreType.DMA
    grad_in, tok, go, h, g, u = pl.pallas_call(
        functools.partial(exchange, n_row, n_col, nc, ns, wire),
        out_shape=[
            jax.ShapeDtypeStruct((rows, feats), BF16),
            jax.ShapeDtypeStruct((feats, panel), BF16),
            jax.ShapeDtypeStruct((panel, feats), BF16),
            jax.ShapeDtypeStruct((hid, panel), BF16),
            jax.ShapeDtypeStruct((panel, hid), BF16),
            jax.ShapeDtypeStruct((panel, hid), BF16),
        ],
        in_specs=[anywhere] * 5,
        out_specs=[pl.BlockSpec(memory_space=pltpu.VMEM)] + [anywhere] * 5,
        scratch_shapes=[
            pltpu.VMEM((2, panel, feats), BF16),
            pltpu.VMEM((nc, feats, chunk), BF16),
            pltpu.VMEM((nc, feats, chunk), BF16),
            pltpu.VMEM((nc, chunk, feats), BF16),
            pltpu.VMEM((nc, 3, panel, chunk), wire),
            pltpu.VMEM((nc, 3, panel, chunk), wire),
            pltpu.VMEM((nc, 3, panel, chunk), wire),
            pltpu.VMEM((nc, 3, panel, chunk), F32),
            pltpu.VMEM((nc, 3, panel, chunk), BF16),
            pltpu.VMEM((panel, feats), F32),
            pltpu.VMEM((n_col, rows, feats), F32),
            pltpu.VMEM((n_col, rows, feats), wire),
            pltpu.VMEM((n_col, rows, feats), wire),
            pltpu.VMEM((feats, panel), BF16),
            pltpu.VMEM((nc, chunk, panel), BF16),
            dma((nc, 3)), dma((2,)), dma((nc, 3)),
            dma((n_col, 2)), dma((n_col, 2)), dma((n_col, 2)), dma((n_col, 2)),
            dma((nc, ns + 1)), dma((nc, ns + 1)), dma((nc, ns + 1)),
            dma((nc, ns + 1)), dma((nc, ns + 1)),
            dma((n_col,)), dma((n_col,)), dma((n_col,)), dma((n_col,)),
        ],
        compiler_params=pltpu.CompilerParams(
            collective_id=0, has_side_effects=True, vmem_limit_bytes=60 * 2**20
        ),
        name="exchange",
    )(tokens, grad_out, gate_weight, up_weight, down_weight)

    nb = max(1, hid // 256)
    whole = lambda i: (0, 0)
    cut = lambda i: (0, i)
    grads = pl.pallas_call(
        outer_products,
        grid=(nb,),
        in_specs=[
            pl.BlockSpec((rows, feats), whole),
            pl.BlockSpec((feats, panel), whole),
            pl.BlockSpec((panel, feats // nb), cut),
            pl.BlockSpec((hid, panel), whole),
            pl.BlockSpec((panel, hid // nb), cut),
            pl.BlockSpec((panel, hid // nb), cut),
        ],
        out_specs=[
            pl.BlockSpec((rows, feats), whole),
            pl.BlockSpec((feats, hid // nb), cut),
            pl.BlockSpec((feats, hid // nb), cut),
            pl.BlockSpec((hid, feats // nb), cut),
        ],
        out_shape=[
            jax.ShapeDtypeStruct((rows, feats), BF16),
            jax.ShapeDtypeStruct((feats, hid), BF16),
            jax.ShapeDtypeStruct((feats, hid), BF16),
            jax.ShapeDtypeStruct((hid, feats), BF16),
        ],
        compiler_params=pltpu.CompilerParams(vmem_limit_bytes=63 * 2**20),
        name="outer_products",
    )(grad_in, tok, go, h, g, u)
    return tuple(grads)


def solution(mesh):
    in_specs = (
        P(("col", "dp"), "row"),
        P(("col", "dp"), "row"),
        P("row", "col"),
        P("row", "col"),
        P("col", "row"),
    )
    out_specs = (
        P(("col", "dp"), "row"),
        P("row", ("col", "dp")),
        P("row", ("col", "dp")),
        P(("col", "dp"), "row"),
    )
    run = functools.partial(body, mesh.shape["row"], mesh.shape["col"])
    return jax.shard_map(run, mesh=mesh, in_specs=in_specs, out_specs=out_specs, check_vma=False)
```

```python
import functools

import jax
import jax.numpy as jnp
from jax import lax
from jax.experimental import pallas as pl
from jax.experimental.pallas import tpu as pltpu
from jax.sharding import PartitionSpec as P

MESH = pl.DeviceIdType.MESH
BF16 = jnp.bfloat16
F32 = jnp.float32


def swiglu_back(gate, up, grad_hidden):
    sig = jax.nn.sigmoid(gate)
    hidden = (gate * sig * up).astype(BF16)
    grad_g = (grad_hidden * up * sig * (1.0 + gate * (1.0 - sig))).astype(BF16)
    grad_u = (grad_hidden * gate * sig).astype(BF16)
    return (hidden, grad_g, grad_u)


def exchange(
    n_row, n_col, nc, ns, wire,
    tok_in, go_in, wg_in, wu_in, wd_in,
    gt_out, tok_out, go_out, h_out, g_out, u_out,
    x_v, wg_v, wu_v, wd_v, send_v, acc_v, mid_v, sum_v, res_v, gt_v, sib_v, peer_src, peer_v,
    turn_v, hid_v, near_v, far_v, gtt_v,
    w_sem, own_sem, out_sem,
    k_send, k_recv, s_send, s_recv,
    p_send, p_recv, m_recv, r_send, r_recv,
    t_send, t_recv, q_send, q_recv,
):
    row, col, dp = lax.axis_index("row"), lax.axis_index("col"), lax.axis_index("dp")
    rows, feats = tok_in.shape
    panel = x_v.shape[1]
    chunk = wg_v.shape[2]
    hid = nc * chunk
    half = n_row // 2
    left = row < half
    inner = jnp.where(left, row + 1, row - 1)
    outer = jnp.where(left, row - 1, row + 1)
    edge = jnp.logical_or(row == 0, row == n_row - 1)
    middle = jnp.logical_or(row == half - 1, row == half)
    off = dp * hid

    first = 2 * rows
    step = (panel - first) // ns
    units = [(0, first)] + [(first + i * step, step) for i in range(ns)]

    def block(k, core):
        return pl.ds(pl.multiple_of((k * 2 + core) * rows, 16), rows)

    def columns(c, base=0):
        return pl.ds(pl.multiple_of(base + c * chunk, 128), chunk)

    def weight_copies(c):
        return (
            pltpu.make_async_copy(wg_in.at[:, columns(c, off)], wg_v.at[c], w_sem.at[c, 0]),
            pltpu.make_async_copy(wu_in.at[:, columns(c, off)], wu_v.at[c], w_sem.at[c, 1]),
            pltpu.make_async_copy(wd_in.at[columns(c, off)], wd_v.at[c], w_sem.at[c, 2]),
        )

    own = [
        pltpu.make_async_copy(src, x_v.at[a, block(0, dp)], own_sem.at[a])
        for a, src in enumerate((tok_in, go_in))
    ]
    for copy in own:
        copy.start()

    def load(c, carry):
        for copy in weight_copies(c):
            copy.start()
        return carry

    lax.fori_loop(0, nc, load, 0)

    def col_at(k):
        return lax.rem(col + k, n_col)

    barrier = pltpu.get_barrier_semaphore()
    for k in range(1, n_col):
        pl.semaphore_signal(barrier, inc=1, device_id=(row, col_at(k), dp), device_id_type=MESH)
    pl.semaphore_signal(barrier, inc=1, device_id=(row, col, 1 - dp), device_id_type=MESH)
    pl.semaphore_signal(barrier, inc=1, device_id=(inner, col, dp), device_id_type=MESH)

    @pl.when(jnp.logical_not(edge))
    def _():
        pl.semaphore_signal(barrier, inc=1, device_id=(outer, col, dp), device_id_type=MESH)
        pl.semaphore_wait(barrier, n_col + 2)

    @pl.when(edge)
    def _():
        pl.semaphore_wait(barrier, n_col + 1)

    def to_peer(k, a):
        return pltpu.make_async_remote_copy(
            src_ref=(tok_in, go_in)[a],
            dst_ref=x_v.at[a, block(n_col - k, dp)],
            send_sem=k_send.at[k, a],
            recv_sem=k_recv.at[k, a],
            device_id=(row, col_at(k), dp),
            device_id_type=MESH,
        )

    def to_sibling(k, a):
        return pltpu.make_async_remote_copy(
            src_ref=(tok_in, go_in)[a] if k == 0 else x_v.at[a, block(k, dp)],
            dst_ref=x_v.at[a, block(k, dp)],
            send_sem=s_send.at[k, a],
            recv_sem=s_recv.at[k, a],
            device_id=(row, col, 1 - dp),
            device_id_type=MESH,
        )

    for a in range(2):
        to_sibling(0, a).start()
    for a in range(2):
        for k in range(1, n_col):
            to_peer(k, a).start()

    def part(ref, c, t):
        return ref.at[c, :, pl.ds(*units[t])]

    def sum_inwards(c, t, into_middle):
        return pltpu.make_async_remote_copy(
            src_ref=part(send_v, c, t),
            dst_ref=part(mid_v if into_middle else acc_v, c, t),
            send_sem=p_send.at[c, t],
            recv_sem=(m_recv if into_middle else p_recv).at[c, t],
            device_id=(inner, col, dp),
            device_id_type=MESH,
        )

    def result_outwards(c, t):
        return pltpu.make_async_remote_copy(
            src_ref=part(res_v, c, t),
            dst_ref=part(res_v, c, t),
            send_sem=r_send.at[c, t],
            recv_sem=r_recv.at[c, t],
            device_id=(outer, col, dp),
            device_id_type=MESH,
        )

    def result_copies(c):
        return [
            pltpu.make_async_copy(hid_v.at[c], h_out.at[columns(c)], out_sem.at[c, 0]),
            pltpu.make_async_copy(res_v.at[c, 1], g_out.at[:, columns(c)], out_sem.at[c, 1]),
            pltpu.make_async_copy(res_v.at[c, 2], u_out.at[:, columns(c)], out_sem.at[c, 2]),
        ]

    gtt_v[...] = jnp.zeros_like(gtt_v)

    def backward(c):
        hid_v[c] = res_v[c, 0].T
        for copy in result_copies(c):
            copy.start()
        gtt_v[...] += jnp.dot(
            wg_v[c], res_v[c, 1].T, preferred_element_type=F32
        ) + jnp.dot(wu_v[c], res_v[c, 2].T, preferred_element_type=F32)

    def finish(c, t):
        sum_inwards(c, t, True).wait_recv()
        at = pl.ds(*units[t])
        h, g, u = swiglu_back(*(sum_v[c, i, at] + mid_v[c, i, at].astype(F32) for i in range(3)))
        res_v[c, 0, at] = h
        res_v[c, 1, at] = g
        res_v[c, 2, at] = u
        if half > 1:
            result_outwards(c, t).start()
        if t == ns:
            backward(c)

    def turned(start, count):
        x = x_v[1, pl.ds(start, count)]
        fill = -count % 128
        if fill:
            x = jnp.concatenate([x, jnp.zeros((fill, feats), BF16)], axis=0)
        return x.T

    def forward(c, start, count, cotangents):
        at = pl.ds(start, count)
        sum_v[c, 0, at] = jnp.dot(x_v[0, at], wg_v[c], preferred_element_type=F32)
        sum_v[c, 1, at] = jnp.dot(x_v[0, at], wu_v[c], preferred_element_type=F32)
        back = jnp.dot(wd_v[c], cotangents[...], preferred_element_type=F32)
        sum_v[c, 2, at] = back.T[:count]

    def send_on(c, t, then):
        at = pl.ds(*units[t])
        if half > 1:

            @pl.when(jnp.logical_not(edge))
            def _():
                sum_inwards(c, t, False).wait_recv()
                sum_v[c, :, at] += acc_v[c, :, at].astype(F32)

        send_v[c, :, at] = sum_v[c, :, at].astype(wire)

        @pl.when(middle)
        def _():
            sum_inwards(c, t, True).start()
            then()

        @pl.when(jnp.logical_not(middle))
        def _():
            sum_inwards(c, t, False).start()

    for copy in own:
        copy.wait()
    for a in range(2):
        to_sibling(0, a).wait_recv()

    near_v[...] = turned(0, first)

    def near(c, carry):
        for copy in weight_copies(c):
            copy.wait()
        forward(c, 0, first, near_v)

        def then():
            @pl.when(c >= ns)
            def _():
                finish(c - ns, 0)

        send_on(c, 0, then)

        @pl.when(c == nc - 2)
        def _():
            for a in range(2):
                for k in range(1, n_col):
                    to_peer(n_col - k, a).wait_recv()
                    to_sibling(k, a).start()

        return carry

    lax.fori_loop(0, nc, near, 0)

    for a in range(2):
        for k in range(1, n_col):
            to_sibling(k, a).wait_recv()

    far_v[...] = turned(first, panel - first)

    def far(c, carry):
        forward(c, first, panel - first, far_v)
        for t in range(1, ns + 1):

            def then(t=t):
                @pl.when(c == 0)
                def _():
                    finish(nc - ns - 1 + t, 0)

                @pl.when(c > 0)
                def _():
                    finish(c - 1, t)

            send_on(c, t, then)
        return carry

    lax.fori_loop(0, nc, far, 0)

    turn_v[...] = x_v[0].T
    x_out = [
        pltpu.make_async_copy(turn_v, tok_out, own_sem.at[0]),
        pltpu.make_async_copy(x_v.at[1], go_out, own_sem.at[1]),
    ]
    for copy in x_out:
        copy.start()

    @pl.when(middle)
    def _():
        for t in range(1, ns + 1):
            finish(nc - 1, t)

    if half > 1:

        @pl.when(jnp.logical_not(middle))
        def _():
            def take(c, t):
                result_outwards(c, t).wait_recv()

                @pl.when(jnp.logical_not(edge))
                def _():
                    result_outwards(c, t).start()

            def take_near(c, carry):
                take(c, 0)
                return carry

            def take_far(c, carry):
                for t in range(1, ns + 1):
                    take(c, t)
                backward(c)
                return carry

            lax.fori_loop(0, nc, take_near, 0)
            lax.fori_loop(0, nc, take_far, 0)

    gt_v[...] = gtt_v[...].T

    def half_to_sibling(k):
        return pltpu.make_async_remote_copy(
            src_ref=gt_v.at[block(k, 1 - dp)],
            dst_ref=sib_v.at[k],
            send_sem=t_send.at[k],
            recv_sem=t_recv.at[k],
            device_id=(row, col, 1 - dp),
            device_id_type=MESH,
        )

    def block_to_owner(k):
        return pltpu.make_async_remote_copy(
            src_ref=peer_src.at[k],
            dst_ref=peer_v.at[k],
            send_sem=q_send.at[k],
            recv_sem=q_recv.at[k],
            device_id=(row, col_at(k), dp),
            device_id_type=MESH,
        )

    order = list(range(1, n_col)) + [0]
    for k in order:
        half_to_sibling(k).start()
    for k in order[:-1]:
        half_to_sibling(k).wait_recv()
        peer_src[k] = (gt_v[block(k, dp), :] + sib_v[k]).astype(wire)
        block_to_owner(k).start()
    half_to_sibling(0).wait_recv()
    total = gt_v[block(0, dp), :] + sib_v[0]
    for k in order[:-1]:
        block_to_owner(k).wait_recv()
        total = total + peer_v[k].astype(F32)
    gt_out[...] = total.astype(BF16)

    for k in order:
        half_to_sibling(k).wait_send()
    for k in order[:-1]:
        block_to_owner(k).wait_send()
    for a in range(2):
        x_out[a].wait()
        for k in range(n_col):
            to_sibling(k, a).wait_send()
            if k > 0:
                to_peer(k, a).wait_send()

    def drain(c, carry):
        for copy in result_copies(c):
            copy.wait()
        for t in range(ns + 1):
            sum_inwards(c, t, False).wait_send()
            if half > 1:

                @pl.when(jnp.logical_not(edge))
                def _():
                    result_outwards(c, t).wait_send()

        return carry

    lax.fori_loop(0, nc, drain, 0)


def outer_products(grad_in, tok, go, h, g, u, grad_tokens, gate_out, up_out, down_out):
    @pl.when(pl.program_id(0) == 0)
    def _():
        grad_tokens[...] = grad_in[...]

    for left, right, out in ((tok, g, gate_out), (tok, u, up_out), (h, go, down_out)):
        width = min(512, right.shape[1])
        for start in range(0, right.shape[1], width):
            at = pl.ds(start, width)
            out[:, at] = jnp.dot(left[...], right[:, at], preferred_element_type=F32).astype(BF16)


def body(n_row, n_col, tokens, grad_out, gate_weight, up_weight, down_weight):
    rows, feats = tokens.shape
    panel = rows * n_col * 2
    hid = gate_weight.shape[1] // 2
    chunk = min(256, hid // 4)
    nc = hid // chunk
    ns = 3 if (panel - 2 * rows) % 48 == 0 else 2
    wire = BF16 if n_row <= 4 else F32
    anywhere = pl.BlockSpec(memory_space=pl.ANY)
    dma = pltpu.SemaphoreType.DMA
    grad_in, tok, go, h, g, u = pl.pallas_call(
        functools.partial(exchange, n_row, n_col, nc, ns, wire),
        out_shape=[
            jax.ShapeDtypeStruct((rows, feats), BF16),
            jax.ShapeDtypeStruct((feats, panel), BF16),
            jax.ShapeDtypeStruct((panel, feats), BF16),
            jax.ShapeDtypeStruct((hid, panel), BF16),
            jax.ShapeDtypeStruct((panel, hid), BF16),
            jax.ShapeDtypeStruct((panel, hid), BF16),
        ],
        in_specs=[anywhere] * 5,
        out_specs=[pl.BlockSpec(memory_space=pltpu.VMEM)] + [anywhere] * 5,
        scratch_shapes=[
            pltpu.VMEM((2, panel, feats), BF16),
            pltpu.VMEM((nc, feats, chunk), BF16),
            pltpu.VMEM((nc, feats, chunk), BF16),
            pltpu.VMEM((nc, chunk, feats), BF16),
            pltpu.VMEM((nc, 3, panel, chunk), wire),
            pltpu.VMEM((nc, 3, panel, chunk), wire),
            pltpu.VMEM((nc, 3, panel, chunk), wire),
            pltpu.VMEM((nc, 3, panel, chunk), F32),
            pltpu.VMEM((nc, 3, panel, chunk), BF16),
            pltpu.VMEM((panel, feats), F32),
            pltpu.VMEM((n_col, rows, feats), F32),
            pltpu.VMEM((n_col, rows, feats), wire),
            pltpu.VMEM((n_col, rows, feats), wire),
            pltpu.VMEM((feats, panel), BF16),
            pltpu.VMEM((nc, chunk, panel), BF16),
            pltpu.VMEM((feats, -(-2 * rows // 128) * 128), BF16),
            pltpu.VMEM((feats, -(-(panel - 2 * rows) // 128) * 128), BF16),
            pltpu.VMEM((feats, panel), F32),
            dma((nc, 3)), dma((2,)), dma((nc, 3)),
            dma((n_col, 2)), dma((n_col, 2)), dma((n_col, 2)), dma((n_col, 2)),
            dma((nc, ns + 1)), dma((nc, ns + 1)), dma((nc, ns + 1)),
            dma((nc, ns + 1)), dma((nc, ns + 1)),
            dma((n_col,)), dma((n_col,)), dma((n_col,)), dma((n_col,)),
        ],
        compiler_params=pltpu.CompilerParams(
            collective_id=0, has_side_effects=True, vmem_limit_bytes=60 * 2**20
        ),
        name="exchange",
    )(tokens, grad_out, gate_weight, up_weight, down_weight)

    nb = max(1, hid // 256)
    whole = lambda i: (0, 0)
    stack = lambda i: (i, 0)
    grads = pl.pallas_call(
        outer_products,
        grid=(nb,),
        in_specs=[
            pl.BlockSpec((rows, feats), whole),
            pl.BlockSpec((feats // nb, panel), stack),
            pl.BlockSpec((panel, feats), whole),
            pl.BlockSpec((hid // nb, panel), stack),
            pl.BlockSpec((panel, hid), whole),
            pl.BlockSpec((panel, hid), whole),
        ],
        out_specs=[
            pl.BlockSpec((rows, feats), whole),
            pl.BlockSpec((feats // nb, hid), stack),
            pl.BlockSpec((feats // nb, hid), stack),
            pl.BlockSpec((hid // nb, feats), stack),
        ],
        out_shape=[
            jax.ShapeDtypeStruct((rows, feats), BF16),
            jax.ShapeDtypeStruct((feats, hid), BF16),
            jax.ShapeDtypeStruct((feats, hid), BF16),
            jax.ShapeDtypeStruct((hid, feats), BF16),
        ],
        compiler_params=pltpu.CompilerParams(vmem_limit_bytes=63 * 2**20),
        name="outer_products",
    )(grad_in, tok, go, h, g, u)
    return tuple(grads)


def solution(mesh):
    in_specs = (
        P(("col", "dp"), "row"),
        P(("col", "dp"), "row"),
        P("row", "col"),
        P("row", "col"),
        P("col", "row"),
    )
    out_specs = (
        P(("col", "dp"), "row"),
        P("row", ("col", "dp")),
        P("row", ("col", "dp")),
        P(("col", "dp"), "row"),
    )
    run = functools.partial(body, mesh.shape["row"], mesh.shape["col"])
    return jax.shard_map(run, mesh=mesh, in_specs=in_specs, out_specs=out_specs, check_vma=False)
```

```python
import functools

import jax
import jax.numpy as jnp
from jax import lax
from jax.experimental import pallas as pl
from jax.experimental.pallas import tpu as pltpu
from jax.sharding import PartitionSpec as P

MESH = pl.DeviceIdType.MESH
BF16 = jnp.bfloat16
F32 = jnp.float32


def swiglu_back(gate, up, grad_hidden):
    sig = jax.nn.sigmoid(gate)
    hidden = (gate * sig * up).astype(BF16)
    grad_g = (grad_hidden * up * sig * (1.0 + gate * (1.0 - sig))).astype(BF16)
    grad_u = (grad_hidden * gate * sig).astype(BF16)
    return (hidden, grad_g, grad_u)


def exchange(
    n_row, n_col, nc, ns, wire,
    tok_in, go_in, wg_in, wu_in, wd_in,
    gt_out, tok_out, go_out, h_out, g_out, u_out,
    x_v, wg_v, wu_v, wd_v, send_v, acc_v, mid_v, sum_v, res_v, gt_v, sib_v, peer_src, peer_v,
    turn_v, hid_v, near_v, far_v, gtt_v,
    w_sem, own_sem, out_sem,
    k_send, k_recv, s_send, s_recv,
    p_send, p_recv, m_recv, r_send, r_recv,
    t_send, t_recv, q_send, q_recv,
):
    row, col, dp = lax.axis_index("row"), lax.axis_index("col"), lax.axis_index("dp")
    rows, feats = tok_in.shape
    panel = x_v.shape[1]
    chunk = wg_v.shape[2]
    hid = nc * chunk
    half = n_row // 2
    left = row < half
    inner = jnp.where(left, row + 1, row - 1)
    outer = jnp.where(left, row - 1, row + 1)
    edge = jnp.logical_or(row == 0, row == n_row - 1)
    middle = jnp.logical_or(row == half - 1, row == half)
    off = dp * hid

    first = 2 * rows
    step = (panel - first) // ns
    units = [(0, first)] + [(first + i * step, step) for i in range(ns)]

    def block(k, core):
        return pl.ds(pl.multiple_of((k * 2 + core) * rows, 16), rows)

    def columns(c, base=0):
        return pl.ds(pl.multiple_of(base + c * chunk, 128), chunk)

    def weight_copies(c):
        return (
            pltpu.make_async_copy(wg_in.at[:, columns(c, off)], wg_v.at[c], w_sem.at[c, 0]),
            pltpu.make_async_copy(wu_in.at[:, columns(c, off)], wu_v.at[c], w_sem.at[c, 1]),
            pltpu.make_async_copy(wd_in.at[columns(c, off)], wd_v.at[c], w_sem.at[c, 2]),
        )

    own = [
        pltpu.make_async_copy(src, x_v.at[a, block(0, dp)], own_sem.at[a])
        for a, src in enumerate((tok_in, go_in))
    ]
    for copy in own:
        copy.start()

    for c in range(2):
        for copy in weight_copies(c):
            copy.start()

    def col_at(k):
        return lax.rem(col + k, n_col)

    barrier = pltpu.get_barrier_semaphore()
    for k in range(1, n_col):
        pl.semaphore_signal(barrier, inc=1, device_id=(row, col_at(k), dp), device_id_type=MESH)
    pl.semaphore_signal(barrier, inc=1, device_id=(row, col, 1 - dp), device_id_type=MESH)
    pl.semaphore_signal(barrier, inc=1, device_id=(inner, col, dp), device_id_type=MESH)

    @pl.when(jnp.logical_not(edge))
    def _():
        pl.semaphore_signal(barrier, inc=1, device_id=(outer, col, dp), device_id_type=MESH)
        pl.semaphore_wait(barrier, n_col + 2)

    @pl.when(edge)
    def _():
        pl.semaphore_wait(barrier, n_col + 1)

    def to_peer(k, a):
        return pltpu.make_async_remote_copy(
            src_ref=(tok_in, go_in)[a],
            dst_ref=x_v.at[a, block(n_col - k, dp)],
            send_sem=k_send.at[k, a],
            recv_sem=k_recv.at[k, a],
            device_id=(row, col_at(k), dp),
            device_id_type=MESH,
        )

    def to_sibling(k, a):
        return pltpu.make_async_remote_copy(
            src_ref=(tok_in, go_in)[a] if k == 0 else x_v.at[a, block(k, dp)],
            dst_ref=x_v.at[a, block(k, dp)],
            send_sem=s_send.at[k, a],
            recv_sem=s_recv.at[k, a],
            device_id=(row, col, 1 - dp),
            device_id_type=MESH,
        )

    for a in range(2):
        to_sibling(0, a).start()
    for a in range(2):
        for k in range(1, n_col):
            to_peer(k, a).start()

    def part(ref, c, t):
        return ref.at[c, :, pl.ds(*units[t])]

    def sum_inwards(c, t, into_middle):
        return pltpu.make_async_remote_copy(
            src_ref=part(send_v, c, t),
            dst_ref=part(mid_v if into_middle else acc_v, c, t),
            send_sem=p_send.at[c, t],
            recv_sem=(m_recv if into_middle else p_recv).at[c, t],
            device_id=(inner, col, dp),
            device_id_type=MESH,
        )

    def result_outwards(c, t):
        return pltpu.make_async_remote_copy(
            src_ref=part(res_v, c, t),
            dst_ref=part(res_v, c, t),
            send_sem=r_send.at[c, t],
            recv_sem=r_recv.at[c, t],
            device_id=(outer, col, dp),
            device_id_type=MESH,
        )

    def result_copies(c):
        return [
            pltpu.make_async_copy(hid_v.at[c], h_out.at[columns(c)], out_sem.at[c, 0]),
            pltpu.make_async_copy(res_v.at[c, 1], g_out.at[:, columns(c)], out_sem.at[c, 1]),
            pltpu.make_async_copy(res_v.at[c, 2], u_out.at[:, columns(c)], out_sem.at[c, 2]),
        ]

    gtt_v[...] = jnp.zeros_like(gtt_v)

    def backward(c):
        hid_v[c] = res_v[c, 0].T
        for copy in result_copies(c):
            copy.start()
        gtt_v[...] += jnp.dot(
            wg_v[c], res_v[c, 1].T, preferred_element_type=F32
        ) + jnp.dot(wu_v[c], res_v[c, 2].T, preferred_element_type=F32)

    def finish(c, t):
        sum_inwards(c, t, True).wait_recv()
        at = pl.ds(*units[t])
        h, g, u = swiglu_back(*(sum_v[c, i, at] + mid_v[c, i, at].astype(F32) for i in range(3)))
        res_v[c, 0, at] = h
        res_v[c, 1, at] = g
        res_v[c, 2, at] = u
        if half > 1:
            result_outwards(c, t).start()
        if t == ns:
            backward(c)

    def turned(start, count):
        x = x_v[1, pl.ds(start, count)]
        fill = -count % 128
        if fill:
            x = jnp.concatenate([x, jnp.zeros((fill, feats), BF16)], axis=0)
        return x.T

    def forward(c, start, count, cotangents):
        at = pl.ds(start, count)
        sum_v[c, 0, at] = jnp.dot(x_v[0, at], wg_v[c], preferred_element_type=F32)
        sum_v[c, 1, at] = jnp.dot(x_v[0, at], wu_v[c], preferred_element_type=F32)
        back = jnp.dot(wd_v[c], cotangents[...], preferred_element_type=F32)
        sum_v[c, 2, at] = back.T[:count]

    def send_on(c, t, then):
        at = pl.ds(*units[t])
        if half > 1:

            @pl.when(jnp.logical_not(edge))
            def _():
                sum_inwards(c, t, False).wait_recv()
                sum_v[c, :, at] += acc_v[c, :, at].astype(F32)

        send_v[c, :, at] = sum_v[c, :, at].astype(wire)

        @pl.when(middle)
        def _():
            sum_inwards(c, t, True).start()
            then()

        @pl.when(jnp.logical_not(middle))
        def _():
            sum_inwards(c, t, False).start()

    for copy in own:
        copy.wait()
    for a in range(2):
        to_sibling(0, a).wait_recv()

    near_v[...] = turned(0, first)

    def near(c, carry):
        @pl.when(c + 2 < nc)
        def _():
            for copy in weight_copies(c + 2):
                copy.start()

        for copy in weight_copies(c):
            copy.wait()
        forward(c, 0, first, near_v)

        def then():
            @pl.when(c >= ns)
            def _():
                finish(c - ns, 0)

        send_on(c, 0, then)

        @pl.when(c == nc - 2)
        def _():
            for a in range(2):
                for k in range(1, n_col):
                    to_peer(n_col - k, a).wait_recv()
                    to_sibling(k, a).start()

        return carry

    lax.fori_loop(0, nc, near, 0)

    for a in range(2):
        for k in range(1, n_col):
            to_sibling(k, a).wait_recv()

    far_v[...] = turned(first, panel - first)

    def far(c, carry):
        forward(c, first, panel - first, far_v)
        for t in range(1, ns + 1):

            def then(t=t):
                @pl.when(c == 0)
                def _():
                    finish(nc - ns - 1 + t, 0)

                @pl.when(c > 0)
                def _():
                    finish(c - 1, t)

            send_on(c, t, then)
        return carry

    lax.fori_loop(0, nc, far, 0)

    turn_v[...] = x_v[0].T
    x_out = [
        pltpu.make_async_copy(turn_v, tok_out, own_sem.at[0]),
        pltpu.make_async_copy(x_v.at[1], go_out, own_sem.at[1]),
    ]
    for copy in x_out:
        copy.start()

    @pl.when(middle)
    def _():
        for t in range(1, ns + 1):
            finish(nc - 1, t)

    if half > 1:

        @pl.when(jnp.logical_not(middle))
        def _():
            def take(c, t):
                result_outwards(c, t).wait_recv()

                @pl.when(jnp.logical_not(edge))
                def _():
                    result_outwards(c, t).start()

            def take_near(c, carry):
                take(c, 0)
                return carry

            def take_far(c, carry):
                for t in range(1, ns + 1):
                    take(c, t)
                backward(c)
                return carry

            lax.fori_loop(0, nc, take_near, 0)
            lax.fori_loop(0, nc, take_far, 0)

    gt_v[...] = gtt_v[...].T

    def half_to_sibling(k):
        return pltpu.make_async_remote_copy(
            src_ref=gt_v.at[block(k, 1 - dp)],
            dst_ref=sib_v.at[k],
            send_sem=t_send.at[k],
            recv_sem=t_recv.at[k],
            device_id=(row, col, 1 - dp),
            device_id_type=MESH,
        )

    def block_to_owner(k):
        return pltpu.make_async_remote_copy(
            src_ref=peer_src.at[k],
            dst_ref=peer_v.at[k],
            send_sem=q_send.at[k],
            recv_sem=q_recv.at[k],
            device_id=(row, col_at(k), dp),
            device_id_type=MESH,
        )

    order = list(range(1, n_col)) + [0]
    for k in order:
        half_to_sibling(k).start()
    for k in order[:-1]:
        half_to_sibling(k).wait_recv()
        peer_src[k] = (gt_v[block(k, dp), :] + sib_v[k]).astype(wire)
        block_to_owner(k).start()
    half_to_sibling(0).wait_recv()
    total = gt_v[block(0, dp), :] + sib_v[0]
    for k in order[:-1]:
        block_to_owner(k).wait_recv()
        total = total + peer_v[k].astype(F32)
    gt_out[...] = total.astype(BF16)

    for k in order:
        half_to_sibling(k).wait_send()
    for k in order[:-1]:
        block_to_owner(k).wait_send()
    for a in range(2):
        x_out[a].wait()
        for k in range(n_col):
            to_sibling(k, a).wait_send()
            if k > 0:
                to_peer(k, a).wait_send()

    def drain(c, carry):
        for copy in result_copies(c):
            copy.wait()
        for t in range(ns + 1):
            sum_inwards(c, t, False).wait_send()
            if half > 1:

                @pl.when(jnp.logical_not(edge))
                def _():
                    result_outwards(c, t).wait_send()

        return carry

    lax.fori_loop(0, nc, drain, 0)


def outer_products(
    nb,
    grad_in, tok, go, h, g, u,
    grad_tokens, gate_out, up_out, down_out,
    tok_v, go_v, h_v, g_v, u_v, gate_v, up_v, down_v, in_sem, out_sem, pass_sem,
):
    through = pltpu.make_async_copy(grad_in, grad_tokens, pass_sem)
    loads = [
        pltpu.make_async_copy(src, dst, in_sem.at[i])
        for i, (src, dst) in enumerate(
            ((tok, tok_v), (g, g_v), (u, u_v), (h, h_v), (go, go_v))
        )
    ]
    for copy in loads:
        copy.start()
    through.start()

    def stores(k, i):
        staged, out = ((gate_v, gate_out), (up_v, up_out), (down_v, down_out))[k]
        count = out.shape[0] // (2 * nb)
        for part in range(2):
            at = pl.ds(pl.multiple_of((2 * i + part) * count, count), count)
            yield pltpu.make_async_copy(staged.at[at], out.at[at], out_sem.at[k, i, part])

    def product(k, left, right, staged):
        count = left.shape[0] // nb
        width = min(512, right.shape[1])

        def step(i, carry):
            at = pl.ds(pl.multiple_of(i * count, count), count)
            for start in range(0, right.shape[1], width):
                cols = pl.ds(start, width)
                staged[at, cols] = jnp.dot(
                    left[at, :], right[:, cols], preferred_element_type=F32
                ).astype(BF16)
            for copy in stores(k, i):
                copy.start()
            return carry

        lax.fori_loop(0, nb, step, 0)

    loads[0].wait()
    loads[1].wait()
    product(0, tok_v, g_v, gate_v)
    loads[2].wait()
    product(1, tok_v, u_v, up_v)
    loads[3].wait()
    loads[4].wait()
    product(2, h_v, go_v, down_v)

    def drain(i, carry):
        for k in range(3):
            for copy in stores(k, i):
                copy.wait()
        return carry

    lax.fori_loop(0, nb, drain, 0)
    through.wait()


def body(n_row, n_col, tokens, grad_out, gate_weight, up_weight, down_weight):
    rows, feats = tokens.shape
    panel = rows * n_col * 2
    hid = gate_weight.shape[1] // 2
    chunk = min(256, hid // 4)
    nc = hid // chunk
    ns = 3 if (panel - 2 * rows) % 48 == 0 else 2
    wire = BF16 if n_row <= 4 else F32
    anywhere = pl.BlockSpec(memory_space=pl.ANY)
    dma = pltpu.SemaphoreType.DMA
    grad_in, tok, go, h, g, u = pl.pallas_call(
        functools.partial(exchange, n_row, n_col, nc, ns, wire),
        out_shape=[
            jax.ShapeDtypeStruct((rows, feats), BF16),
            jax.ShapeDtypeStruct((feats, panel), BF16),
            jax.ShapeDtypeStruct((panel, feats), BF16),
            jax.ShapeDtypeStruct((hid, panel), BF16),
            jax.ShapeDtypeStruct((panel, hid), BF16),
            jax.ShapeDtypeStruct((panel, hid), BF16),
        ],
        in_specs=[anywhere] * 5,
        out_specs=[pl.BlockSpec(memory_space=pltpu.VMEM)] + [anywhere] * 5,
        scratch_shapes=[
            pltpu.VMEM((2, panel, feats), BF16),
            pltpu.VMEM((nc, feats, chunk), BF16),
            pltpu.VMEM((nc, feats, chunk), BF16),
            pltpu.VMEM((nc, chunk, feats), BF16),
            pltpu.VMEM((nc, 3, panel, chunk), wire),
            pltpu.VMEM((nc, 3, panel, chunk), wire),
            pltpu.VMEM((nc, 3, panel, chunk), wire),
            pltpu.VMEM((nc, 3, panel, chunk), F32),
            pltpu.VMEM((nc, 3, panel, chunk), BF16),
            pltpu.VMEM((panel, feats), F32),
            pltpu.VMEM((n_col, rows, feats), F32),
            pltpu.VMEM((n_col, rows, feats), wire),
            pltpu.VMEM((n_col, rows, feats), wire),
            pltpu.VMEM((feats, panel), BF16),
            pltpu.VMEM((nc, chunk, panel), BF16),
            pltpu.VMEM((feats, -(-2 * rows // 128) * 128), BF16),
            pltpu.VMEM((feats, -(-(panel - 2 * rows) // 128) * 128), BF16),
            pltpu.VMEM((feats, panel), F32),
            dma((nc, 3)), dma((2,)), dma((nc, 3)),
            dma((n_col, 2)), dma((n_col, 2)), dma((n_col, 2)), dma((n_col, 2)),
            dma((nc, ns + 1)), dma((nc, ns + 1)), dma((nc, ns + 1)),
            dma((nc, ns + 1)), dma((nc, ns + 1)),
            dma((n_col,)), dma((n_col,)), dma((n_col,)), dma((n_col,)),
        ],
        compiler_params=pltpu.CompilerParams(
            collective_id=0, has_side_effects=True, vmem_limit_bytes=60 * 2**20
        ),
        name="exchange",
    )(tokens, grad_out, gate_weight, up_weight, down_weight)

    nb = max(1, hid // 256)
    grads = pl.pallas_call(
        functools.partial(outer_products, nb),
        in_specs=[anywhere] * 6,
        out_specs=[anywhere] * 4,
        scratch_shapes=[
            pltpu.VMEM((feats, panel), BF16),
            pltpu.VMEM((panel, feats), BF16),
            pltpu.VMEM((hid, panel), BF16),
            pltpu.VMEM((panel, hid), BF16),
            pltpu.VMEM((panel, hid), BF16),
            pltpu.VMEM((feats, hid), BF16),
            pltpu.VMEM((feats, hid), BF16),
            pltpu.VMEM((hid, feats), BF16),
            dma((5,)), dma((3, nb, 2)), dma,
        ],
        out_shape=[
            jax.ShapeDtypeStruct((rows, feats), BF16),
            jax.ShapeDtypeStruct((feats, hid), BF16),
            jax.ShapeDtypeStruct((feats, hid), BF16),
            jax.ShapeDtypeStruct((hid, feats), BF16),
        ],
        compiler_params=pltpu.CompilerParams(vmem_limit_bytes=63 * 2**20),
        name="outer_products",
    )(grad_in, tok, go, h, g, u)
    return tuple(grads)


def solution(mesh):
    in_specs = (
        P(("col", "dp"), "row"),
        P(("col", "dp"), "row"),
        P("row", "col"),
        P("row", "col"),
        P("col", "row"),
    )
    out_specs = (
        P(("col", "dp"), "row"),
        P("row", ("col", "dp")),
        P("row", ("col", "dp")),
        P(("col", "dp"), "row"),
    )
    run = functools.partial(body, mesh.shape["row"], mesh.shape["col"])
    return jax.shard_map(run, mesh=mesh, in_specs=in_specs, out_specs=out_specs, check_vma=False)
```
